768 devices in a mesh: dp: 192 (over y, z, core), proto: 4 (over x).
Axes of the slice: x: 4, y: 8, z: 12, core: 2. Of those that a mesh axis runs over, the one named last changes fastest.
Arguments:
- tokens: bfloat16 [24576, 256], P('dp'), may hold values from -48 to 48
- teacher_protos: float32 [4, 12288, 256], P('proto', 'dp'), may hold values from -48 to 48
- student_protos: float32 [4, 12288, 256], P('proto', 'dp'), may hold values from -48 to 48
- momentum: float32 [1], replicated, may hold values from 0.5 to 0.95
Outputs:
- teacher_next: float32 [4, 12288, 256], P('proto', 'dp')
- targets: bfloat16 [24576, 49152], P('dp', 'proto')
The draws below stay inside these ranges and needn't reach their ends.
All inputs are finite; a program needn't handle non-finite values.
Results may differ from the reference program's by a relative error of at most 0.0054.
Values may be sent and summed in bfloat16 or wider, within the bound.
A program may use at most 32 MiB of HBM per device.

```python
import math
import jax
import jax.numpy as jnp
from jax import lax

BOT = 256
TOK_DEV = 128
ITERS = 3
GROUPS = 4
KL = 12288
TOKENS = 24576


cluster_count = 48


pool_width = 3


entry_limit = 48.0


def shared_layout(key):
    centre_key, column_key, member_key, length_key = jax.random.split(key, 4)
    centres = jax.random.normal(centre_key, (cluster_count, BOT), jnp.float32)
    column_scale = jnp.exp(jax.random.uniform(column_key, (BOT,), jnp.float32, math.log(0.4), math.log(4.0)))
    proto_cluster = jax.random.randint(member_key, (GROUPS, KL), 0, cluster_count)
    proto_length = jnp.exp(jax.random.uniform(length_key, (GROUPS, KL, 1), jnp.float32, math.log(0.4), math.log(4.0)))
    return (centres, column_scale, proto_cluster, proto_length)


def popular_cluster(key, count):
    candidates = jax.random.randint(key, (3, count), 0, cluster_count)
    return jnp.min(candidates, axis=0)


def build_protos(layout, jitter):
    centres, column_scale, proto_cluster, proto_length = layout
    values = (centres[proto_cluster] + 0.75 * jitter) * column_scale * proto_length
    return jnp.clip(values, -entry_limit, entry_limit)


def draw_tokens(key, part):
    centres, column_scale, proto_cluster, proto_length = shared_layout(key)
    key = jax.random.fold_in(key, 7)
    pick_key, slot_key, level_key, length_key, jitter_key = jax.random.split(key, 5)
    block_total = TOKENS // TOK_DEV
    block_pool = popular_cluster(pick_key, block_total * pool_width).reshape(block_total, pool_width)
    slot_pick = jax.random.randint(slot_key, (block_total, TOK_DEV), 0, pool_width)
    token_cluster = jnp.take_along_axis(block_pool, slot_pick, axis=1).reshape(TOKENS)
    level = jax.random.uniform(level_key, (TOKENS, 1), jnp.float32, 0.5, 1.5)
    jitter = jax.random.normal(jitter_key, (TOKENS, BOT), jnp.float32)
    token_length = jnp.exp(jax.random.uniform(length_key, (TOKENS, 1), jnp.float32, math.log(0.4), math.log(4.0)))
    values = (centres[token_cluster] + level * jitter) * column_scale * token_length
    return jnp.clip(values, -entry_limit, entry_limit).astype(jnp.bfloat16)


def draw_teacher_protos(key, part):
    layout = shared_layout(key)
    key = jax.random.fold_in(key, 11)
    jitter = jax.random.normal(key, (GROUPS, KL, BOT), jnp.float32)
    return build_protos(layout, jitter)


def draw_student_protos(key, part):
    layout = shared_layout(key)
    key = jax.random.fold_in(key, 13)
    jitter = jax.random.normal(key, (GROUPS, KL, BOT), jnp.float32)
    return build_protos(layout, jitter)


def setup_inputs(seed: int = 0) -> dict:
    key_list = jax.random.split(jax.random.key(seed), 5)
    tokens = draw_tokens(jax.random.fold_in(key_list[4], 71), 0)
    teacher_protos = draw_teacher_protos(jax.random.fold_in(key_list[4], 71), 0)
    student_protos = draw_student_protos(jax.random.fold_in(key_list[4], 71), 0)
    momentum = jnp.clip(jax.random.uniform(key_list[3], (1,), jnp.float32, 0.5, 0.95), 0.5, 0.95)
    return dict(tokens=tokens, teacher_protos=teacher_protos, student_protos=student_protos, momentum=momentum)


TEACHER_TEMP = 0.07

def unit_rows(matrix):
    return matrix / jnp.sqrt(lax.optimization_barrier(jnp.sum(matrix * matrix, axis=-1, keepdims=True)) + 1e-06)

def reference(tokens, teacher_protos, student_protos, momentum):
    keep_rate = momentum[0]
    teacher_next = keep_rate * teacher_protos + (1.0 - keep_rate) * student_protos
    width_all = teacher_next.shape[0] * teacher_next.shape[1]
    unit_protos = unit_rows(teacher_next.reshape(width_all, teacher_next.shape[2])).astype(jnp.bfloat16)
    unit_tokens = unit_rows(tokens.astype(jnp.float32)).astype(jnp.bfloat16)
    block_count = unit_tokens.shape[0] // TOK_DEV

    def score_block(block_tokens):
        scores = lax.dot_general(block_tokens, unit_protos, (((1,), (1,)), ((), ())), preferred_element_type=jnp.float32)
        return jnp.exp(scores / TEACHER_TEMP)
    base = lax.map(score_block, unit_tokens.reshape(block_count, TOK_DEV, unit_tokens.shape[1]))
    base = base.reshape(unit_tokens.shape[0], width_all)
    token_scale = jnp.ones((unit_tokens.shape[0],), jnp.float32)
    proto_scale = jnp.ones((width_all,), jnp.float32)
    for repeat in range(ITERS):
        proto_scale = 1.0 / jnp.dot(token_scale, base, precision=lax.Precision.HIGHEST)
        token_scale = 1.0 / jnp.dot(base, proto_scale, precision=lax.Precision.HIGHEST)

    def target_block(pair):
        block_base, block_scale = pair
        return ((width_all * block_scale)[:, None] * block_base * proto_scale[None, :]).astype(jnp.bfloat16)
    targets = lax.map(target_block, (base.reshape(block_count, TOK_DEV, width_all), token_scale.reshape(block_count, TOK_DEV)))
    return (teacher_next, targets.reshape(unit_tokens.shape[0], width_all))
```

```python
import functools

import jax
import jax.numpy as jnp
from jax import lax
from jax.experimental import pallas as pl
from jax.experimental.pallas import tpu as pltpu
from jax.sharding import PartitionSpec as P

ITERS = 3
TEACHER_TEMP = 0.07
MESH = pl.DeviceIdType.MESH
F32 = jnp.float32
BF16 = jnp.bfloat16


def unit_rows(m):
    return m / jnp.sqrt(jnp.sum(m * m, axis=-1, keepdims=True) + 1e-06)


def nt_dot(a, b):
    return lax.dot_general(a, b, (((1,), (1,)), ((), ())), preferred_element_type=F32)


def two_term_rows(v):
    n = v.shape[1]
    x = jnp.broadcast_to(v, (16, n))
    hi = x.astype(BF16).astype(F32)
    row = lax.broadcasted_iota(jnp.int32, (16, n), 0)
    return jnp.where(row == 0, hi, jnp.where(row == 1, x - hi, 0.0)).astype(BF16)


def far_first(offsets, dist):
    return sorted(offsets, key=lambda o: (-dist(o), o))


def ring_dist(d, n):
    return min(d, n - d)


def sinkhorn_kernel(
    X, Y, Z,
    mom_ref, tok_ref, tea_ref, stu_ref,
    g_ref, ps_ref, ts_ref,
    pc, tc, base, csend, cpair, zbuf, rsend, xbuf, tbuf,
    own_sem, zg_send, zg_recv, tg_send, tg_recv, sf_send, sf_recv,
    c_send, c_recv, z_send, z_recv, r_send, r_recv, p_send, p_recv,
    ring_send, ring_recv, sib_send, sib_recv,
):
    x = lax.axis_index("proto")
    dp = lax.axis_index("dp")
    y, z, c = dp // (2 * Z), (dp // 2) % Z, dp % 2

    def at(xx, yy, zz, cc):
        return {"dp": (yy * Z + zz) * 2 + cc, "proto": xx}

    sibling = at(x, y, z, 1 - c)
    z_off = far_first(range(1, Z), lambda d: ring_dist(d, Z))
    y_off = far_first(range(1, Y), lambda d: ring_dist(d, Y))
    xy_off = far_first(
        [(dx, dy) for dx in range(X) for dy in range(Y) if (dx, dy) != (0, 0)],
        lambda o: ring_dist(o[0], X) + ring_dist(o[1], Y),
    )
    z_dev = [at(x, y, (z + d) % Z, c) for d in z_off]
    y_dev = [at(x, (y + d) % Y, z, c) for d in y_off]
    xy_dev = [at((x + dx) % X, (y + dy) % Y, z, c) for dx, dy in xy_off]

    barrier = pltpu.get_barrier_semaphore()
    greeted = [sibling] + z_dev + xy_dev
    for d in greeted:
        pl.semaphore_signal(barrier, inc=1, device_id=d, device_id_type=MESH)

    keep = mom_ref[0]
    pc[z, c] = unit_rows(keep * tea_ref[0] + (1.0 - keep) * stu_ref[0]).astype(BF16)
    tc[y] = unit_rows(tok_ref[...].astype(F32)).astype(BF16)
    pl.semaphore_wait(barrier, len(greeted))

    def send(src, dst, s, r, d):
        copy = pltpu.make_async_remote_copy(
            src_ref=src, dst_ref=dst, send_sem=s, recv_sem=r, device_id=d, device_id_type=MESH
        )
        copy.start()
        return copy

    def wait_bytes(ref, sem):
        pltpu.make_async_copy(ref, ref, sem).wait()

    for d in z_dev:
        send(pc.at[z, c], pc.at[z, c], zg_send, zg_recv, d)
    for d in y_dev:
        send(tc.at[y], tc.at[y], tg_send, tg_recv, d)
    wait_bytes(pc.at[0 : Z - 1, 0], zg_recv)
    swap = send(pc.at[:, c], pc.at[:, c], sf_send, sf_recv, sibling)

    up, down = at(x, (y + 1) % Y, z, c), at(x, (y + Y - 1) % Y, z, c)
    up_steps, down_steps = Y // 2, Y - 1 - Y // 2
    sends, sib = [], []

    def ring_step(s):
        if s <= up_steps:
            b = (y - s + 1 + Y) % Y
            src = pc.at[:, c] if s == 1 else g_ref.at[b, :, c]
            i = s - 1
            sends.append(send(src, g_ref.at[b, :, c], ring_send.at[i], ring_recv.at[i], up))
        if s <= down_steps:
            b = (y + s - 1) % Y
            src = pc.at[:, c] if s == 1 else g_ref.at[b, :, c]
            i = up_steps + s - 1
            sends.append(send(src, g_ref.at[b, :, c], ring_send.at[i], ring_recv.at[i], down))

    def ring_arrive(s):
        if s <= up_steps:
            b, i = (y - s + Y) % Y, s - 1
            wait_bytes(g_ref.at[b, :, c], ring_recv.at[i])
            sib.append(send(g_ref.at[b, :, c], g_ref.at[b, :, c], sib_send.at[i], sib_recv.at[i], sibling))
        if s <= down_steps:
            b, i = (y + s) % Y, up_steps + s - 1
            wait_bytes(g_ref.at[b, :, c], ring_recv.at[i])
            sib.append(send(g_ref.at[b, :, c], g_ref.at[b, :, c], sib_send.at[i], sib_recv.at[i], sibling))

    ring_step(1)
    wait_bytes(tc.at[0 : Y - 1], tg_recv)
    swap.wait_recv()
    own = pltpu.make_async_copy(pc, g_ref.at[y], own_sem)
    own.start()

    tdev = tc.shape[1]
    kb = base.shape[1]
    protos = pc[...].reshape(kb, pc.shape[3])

    def score(i, acc):
        b = jnp.exp(nt_dot(tc[i], protos) / TEACHER_TEMP)
        base[pl.ds(pl.multiple_of(i * tdev, tdev), tdev), :] = b.astype(BF16)
        return acc + jnp.sum(b, axis=0, keepdims=True)

    cols = lax.fori_loop(0, Y, score, jnp.zeros((1, kb), F32))

    for it in range(ITERS):
        csend[it, 0] = cols
        pair = send(csend.at[it, 0], cpair.at[it], c_send.at[it], c_recv.at[it], sibling)
        pair.wait_recv()
        cols = cols + cpair[it]
        csend[it, 1] = cols
        for i, d in enumerate(z_dev):
            send(csend.at[it, 1], zbuf.at[it, i], z_send.at[it], z_recv.at[it], d)
        wait_bytes(zbuf.at[it], z_recv.at[it])
        protos_scale = 1.0 / (cols + jnp.sum(zbuf[it], axis=0))
        if it == ITERS - 1:
            ps_ref[y] = protos_scale
            for d in y_dev:
                send(ps_ref.at[y], ps_ref.at[y], p_send, p_recv, d)
        rows = jnp.sum(nt_dot(two_term_rows(protos_scale), base[...]), axis=0, keepdims=True)
        rsend[it] = rows
        for i, d in enumerate(xy_dev):
            send(rsend.at[it], xbuf.at[it, i], r_send.at[it], r_recv.at[it], d)
        if 2 * it + 1 <= up_steps:
            ring_arrive(2 * it + 1)
            ring_step(2 * it + 2)
        wait_bytes(xbuf.at[it], r_recv.at[it])
        token_scale = 1.0 / (rows + jnp.sum(xbuf[it], axis=0))
        if it < ITERS - 1:
            cols = jnp.sum(
                jnp.dot(two_term_rows(token_scale), base[...], preferred_element_type=F32),
                axis=0,
                keepdims=True,
            )
            if 2 * it + 2 <= up_steps:
                ring_arrive(2 * it + 2)
                ring_step(2 * it + 3)
        else:
            for i in range(Y):
                tbuf[i] = token_scale[:, i * tdev : (i + 1) * tdev]
            ts_ref[...] = tbuf[y]
        pair.wait_send()
        wait_bytes(zbuf.at[it], z_send.at[it])
        wait_bytes(xbuf.at[it], r_send.at[it])

    wait_bytes(ps_ref.at[0 : Y - 1], p_recv)
    wait_bytes(ps_ref.at[0 : Y - 1], p_send)
    wait_bytes(pc.at[0 : Z - 1, 0], zg_send)
    wait_bytes(tc.at[0 : Y - 1], tg_send)
    own.wait()
    swap.wait_send()
    for copy in sends:
        copy.wait_send()
    for copy in sib:
        copy.wait()


def target_kernel(
    width, mom_ref, tok_ref, tea_ref, stu_ref, g_ref, ps_ref, ts_ref, next_ref, out_ref, unit, scale
):
    @pl.when(pl.program_id(0) == 0)
    def _():
        keep = mom_ref[0]
        next_ref[...] = keep * tea_ref[...] + (1.0 - keep) * stu_ref[...]
        unit[...] = unit_rows(tok_ref[...].astype(F32)).astype(BF16)
        n = ts_ref.shape[1]
        scale[...] = jnp.transpose(jnp.broadcast_to(width * ts_ref[...], (n, n)))

    b = jnp.exp(nt_dot(unit[...], g_ref[0]) / TEACHER_TEMP)
    out_ref[...] = (scale[:, 0:1] * b * ps_ref[0]).astype(BF16)


def body(X, Y, Z, tokens, teacher_protos, student_protos, momentum):
    tdev, width = tokens.shape
    kdev = teacher_protos.shape[1]
    kb, tb = 2 * Z * kdev, Y * tdev
    n_up = Y - 1
    dma = pltpu.SemaphoreType.DMA
    vmem = pl.BlockSpec(memory_space=pltpu.VMEM)
    smem = pl.BlockSpec(memory_space=pltpu.SMEM)
    groups, proto_scale, token_scale = pl.pallas_call(
        functools.partial(sinkhorn_kernel, X, Y, Z),
        out_shape=(
            jax.ShapeDtypeStruct((Y, Z, 2, kdev, width), BF16),
            jax.ShapeDtypeStruct((Y, 1, kb), F32),
            jax.ShapeDtypeStruct((1, tdev), F32),
        ),
        in_specs=[smem, vmem, vmem, vmem],
        out_specs=(pl.BlockSpec(memory_space=pl.ANY), vmem, vmem),
        scratch_shapes=[
            pltpu.VMEM((Z, 2, kdev, width), BF16),
            pltpu.VMEM((Y, tdev, width), BF16),
            pltpu.VMEM((tb, kb), BF16),
            pltpu.VMEM((ITERS, 2, 1, kb), F32),
            pltpu.VMEM((ITERS, 1, kb), F32),
            pltpu.VMEM((ITERS, Z - 1, 1, kb), F32),
            pltpu.VMEM((ITERS, 1, tb), F32),
            pltpu.VMEM((ITERS, X * Y - 1, 1, tb), F32),
            pltpu.VMEM((Y, 1, tdev), F32),
            dma, dma, dma, dma, dma, dma, dma,
            dma((ITERS,)), dma((ITERS,)), dma((ITERS,)), dma((ITERS,)), dma((ITERS,)), dma((ITERS,)),
            dma, dma,
            dma((n_up,)), dma((n_up,)), dma((n_up,)), dma((n_up,)),
        ],
        compiler_params=pltpu.CompilerParams(
            collective_id=0, has_side_effects=True, vmem_limit_bytes=40 * 2**20
        ),
        name="sinkhorn",
    )(momentum, tokens, teacher_protos, student_protos)
    groups = groups.reshape(Y, kb, width)
    return pl.pallas_call(
        functools.partial(target_kernel, float(X * Y * kb)),
        grid=(Y,),
        out_shape=(
            jax.ShapeDtypeStruct(teacher_protos.shape, F32),
            jax.ShapeDtypeStruct((tdev, Y * kb), BF16),
        ),
        in_specs=[
            smem,
            pl.BlockSpec((tdev, width), lambda i: (0, 0)),
            pl.BlockSpec((1, kdev, width), lambda i: (0, 0, 0)),
            pl.BlockSpec((1, kdev, width), lambda i: (0, 0, 0)),
            pl.BlockSpec((1, kb, width), lambda i: (i, 0, 0)),
            pl.BlockSpec((1, 1, kb), lambda i: (i, 0, 0)),
            pl.BlockSpec((1, tdev), lambda i: (0, 0)),
        ],
        out_specs=(
            pl.BlockSpec((1, kdev, width), lambda i: (0, 0, 0)),
            pl.BlockSpec((tdev, kb), lambda i: (0, i)),
        ),
        scratch_shapes=[pltpu.VMEM((tdev, width), BF16), pltpu.VMEM((tdev, tdev), F32)],
        compiler_params=pltpu.CompilerParams(vmem_limit_bytes=40 * 2**20),
        name="targets",
    )(momentum, tokens, teacher_protos, student_protos, groups, proto_scale, token_scale)


def build(mesh, X, Y, Z):
    return jax.shard_map(
        functools.partial(body, X, Y, Z),
        mesh=mesh,
        in_specs=(P("dp", None), P("proto", "dp", None), P("proto", "dp", None), P()),
        out_specs=(P("proto", "dp", None), P("dp", "proto")),
        check_vma=False,
    )


def solution(mesh):
    return build(mesh, mesh.shape["proto"], 8, mesh.shape["dp"] // 16)
```

```python
import functools

import jax
import jax.numpy as jnp
from jax import lax
from jax.experimental import pallas as pl
from jax.experimental.pallas import tpu as pltpu
from jax.sharding import PartitionSpec as P

ITERS = 3
TEACHER_TEMP = 0.07
MESH = pl.DeviceIdType.MESH
F32 = jnp.float32
BF16 = jnp.bfloat16


def unit_rows(m):
    return m / jnp.sqrt(jnp.sum(m * m, axis=-1, keepdims=True) + 1e-06)


def nt_dot(a, b):
    return lax.dot_general(a, b, (((1,), (1,)), ((), ())), preferred_element_type=F32)


def two_term_rows(v):
    n = v.shape[1]
    x = jnp.broadcast_to(v, (16, n))
    hi = x.astype(BF16).astype(F32)
    row = lax.broadcasted_iota(jnp.int32, (16, n), 0)
    return jnp.where(row == 0, hi, jnp.where(row == 1, x - hi, 0.0)).astype(BF16)


def far_first(offsets, dist):
    return sorted(offsets, key=lambda o: (-dist(o), o))


def ring_dist(d, n):
    return min(d, n - d)


def sinkhorn_kernel(
    X, Y, Z,
    mom_ref, tok_hbm, tea_hbm, stu_hbm,
    out_base, ps_ref, ts_ref, next_ref,
    tok_ref, tea_ref, stu_ref, g_ref, pc, tc, base, csend, cpair, zbuf, rsend, xbuf, tbuf,
    in_sem, zg_send, zg_recv, tg_send, tg_recv, sf_send, sf_recv,
    c_send, c_recv, z_send, z_recv, r_send, r_recv, p_send, p_recv,
    ring_send, ring_recv, sib_send, sib_recv,
):
    x = lax.axis_index("proto")
    dp = lax.axis_index("dp")
    y, z, c = dp // (2 * Z), (dp // 2) % Z, dp % 2

    def at(xx, yy, zz, cc):
        return {"dp": (yy * Z + zz) * 2 + cc, "proto": xx}

    sibling = at(x, y, z, 1 - c)
    z_off = far_first(range(1, Z), lambda d: ring_dist(d, Z))
    y_off = far_first(range(1, Y), lambda d: ring_dist(d, Y))
    xy_off = far_first(
        [(dx, dy) for dx in range(X) for dy in range(Y) if (dx, dy) != (0, 0)],
        lambda o: ring_dist(o[0], X) + ring_dist(o[1], Y),
    )
    z_dev = [at(x, y, (z + d) % Z, c) for d in z_off]
    y_dev = [at(x, (y + d) % Y, z, c) for d in y_off]
    xy_dev = [at((x + dx) % X, (y + dy) % Y, z, c) for dx, dy in xy_off]

    loads = [
        pltpu.make_async_copy(src, dst, in_sem.at[i])
        for i, (src, dst) in enumerate([(tea_hbm, tea_ref), (stu_hbm, stu_ref), (tok_hbm, tok_ref)])
    ]
    for load in loads:
        load.start()

    barrier = pltpu.get_barrier_semaphore()
    greeted = [sibling] + z_dev + xy_dev
    for d in greeted:
        pl.semaphore_signal(barrier, inc=1, device_id=d, device_id_type=MESH)

    keep = mom_ref[0]
    for load in loads:
        load.wait()
    teacher_next = keep * tea_ref[0] + (1.0 - keep) * stu_ref[0]
    next_ref[0] = teacher_next
    pc[z, c] = unit_rows(teacher_next).astype(BF16)
    tc[y] = unit_rows(tok_ref[...].astype(F32)).astype(BF16)
    pl.semaphore_wait(barrier, len(greeted))

    def send(src, dst, s, r, d):
        copy = pltpu.make_async_remote_copy(
            src_ref=src, dst_ref=dst, send_sem=s, recv_sem=r, device_id=d, device_id_type=MESH
        )
        copy.start()
        return copy

    def wait_bytes(ref, sem):
        pltpu.make_async_copy(ref, ref, sem).wait()

    for d in z_dev:
        send(pc.at[z, c], pc.at[z, c], zg_send, zg_recv, d)
    for d in y_dev:
        send(tc.at[y], tc.at[y], tg_send, tg_recv, d)
    wait_bytes(pc.at[0 : Z - 1, 0], zg_recv)
    swap = send(pc.at[:, c], pc.at[:, c], sf_send, sf_recv, sibling)

    up, down = at(x, (y + 1) % Y, z, c), at(x, (y + Y - 1) % Y, z, c)
    last, zh = Y // 2, Z // 2
    sends, sib = [], {}

    def ring_parts(s):
        if s < last:
            yield s - 1, up, (y - s + 1 + Y) % Y, (y - s + Y) % Y, slice(0, Z)
            yield last + s - 1, down, (y + s - 1) % Y, (y + s) % Y, slice(0, Z)
        elif s == last:
            yield s - 1, up, (y - s + 1 + Y) % Y, (y - s + Y) % Y, slice(0, zh)
            yield last + s - 1, down, (y + s - 1) % Y, (y + s) % Y, slice(zh, Z)

    def ring_step(s):
        for i, to, b, _, rows in ring_parts(s):
            src = pc.at[rows, c] if s == 1 else g_ref.at[b, rows, c]
            sends.append(send(src, g_ref.at[b, rows, c], ring_send.at[i], ring_recv.at[i], to))

    def ring_arrive(s):
        for i, _, _, b, rows in ring_parts(s):
            part = g_ref.at[b, rows, c]
            wait_bytes(part, ring_recv.at[i])
            sib[i] = send(part, part, sib_send.at[i], sib_recv.at[i], sibling)

    def ring_block(s):
        for i, _, _, b, _ in ring_parts(s):
            sib[i].wait_recv()
        for b in [(y - s + Y) % Y] * (s <= last) + [(y + s) % Y] * (s < last):
            block_base(b, g_ref[b])

    ring_step(1)
    wait_bytes(tc.at[0 : Y - 1], tg_recv)
    swap.wait_recv()

    tdev = tc.shape[1]
    kb = base.shape[1]
    protos = pc[...].reshape(kb, pc.shape[3])

    def block_base(b, block):
        scores = nt_dot(tc[y], block.reshape(kb, pc.shape[3]))
        out_base[b] = jnp.exp(scores / TEACHER_TEMP)

    def score(i, acc):
        b = jnp.exp(nt_dot(tc[i], protos) / TEACHER_TEMP)
        base[pl.ds(pl.multiple_of(i * tdev, tdev), tdev), :] = b.astype(BF16)
        return acc + jnp.sum(b, axis=0, keepdims=True)

    cols = lax.fori_loop(0, Y, score, jnp.zeros((1, kb), F32))

    for it in range(ITERS):
        csend[it, 0] = cols
        pair = send(csend.at[it, 0], cpair.at[it], c_send.at[it], c_recv.at[it], sibling)
        pair.wait_recv()
        cols = cols + cpair[it]
        csend[it, 1] = cols
        for i, d in enumerate(z_dev):
            send(csend.at[it, 1], zbuf.at[it, i], z_send.at[it], z_recv.at[it], d)
        if it == 0:
            block_base(y, pc[...])
        if it == 1:
            ring_block(1)
        if it == 2:
            ring_arrive(3)
            ring_step(4)
            ring_block(2)
        wait_bytes(zbuf.at[it], z_recv.at[it])
        protos_scale = 1.0 / (cols + jnp.sum(zbuf[it], axis=0))
        if it == ITERS - 1:
            ps_ref[y] = protos_scale
            for d in y_dev:
                send(ps_ref.at[y], ps_ref.at[y], p_send, p_recv, d)
        rows = jnp.sum(nt_dot(two_term_rows(protos_scale), base[...]), axis=0, keepdims=True)
        rsend[it] = rows
        for i, d in enumerate(xy_dev):
            send(rsend.at[it], xbuf.at[it, i], r_send.at[it], r_recv.at[it], d)
        if it == 1:
            ring_arrive(2)
            ring_step(3)
        if it == 2:
            ring_arrive(4)
            ring_block(3)
            ring_block(4)
        wait_bytes(xbuf.at[it], r_recv.at[it])
        token_scale = 1.0 / (rows + jnp.sum(xbuf[it], axis=0))
        if it < ITERS - 1:
            cols = jnp.sum(
                jnp.dot(two_term_rows(token_scale), base[...], preferred_element_type=F32),
                axis=0,
                keepdims=True,
            )
            if it == 0:
                ring_arrive(1)
                ring_step(2)
        else:
            for i in range(Y):
                tbuf[i] = token_scale[:, i * tdev : (i + 1) * tdev]
            ts_ref[...] = tbuf[y]
        pair.wait_send()
        wait_bytes(zbuf.at[it], z_send.at[it])
        wait_bytes(xbuf.at[it], r_send.at[it])

    wait_bytes(ps_ref.at[0 : Y - 1], p_recv)
    wait_bytes(ps_ref.at[0 : Y - 1], p_send)
    wait_bytes(pc.at[0 : Z - 1, 0], zg_send)
    wait_bytes(tc.at[0 : Y - 1], tg_send)
    swap.wait_send()
    for copy in sends:
        copy.wait_send()
    for copy in sib.values():
        copy.wait_send()


def target_kernel(width, new_ref, base_ref, ps_ref, ts_ref, next_ref, out_ref, scale):
    @pl.when(pl.program_id(0) == 0)
    def _():
        next_ref[...] = new_ref[...]
        n = ts_ref.shape[1]
        scale[...] = jnp.transpose(jnp.broadcast_to(width * ts_ref[...], (n, n)))

    out_ref[...] = (scale[:, 0:1] * base_ref[0] * ps_ref[0]).astype(BF16)


def body(X, Y, Z, tokens, teacher_protos, student_protos, momentum):
    tdev, width = tokens.shape
    kdev = teacher_protos.shape[1]
    kb, tb = 2 * Z * kdev, Y * tdev
    n_ring = 2 * (Y // 2)
    dma = pltpu.SemaphoreType.DMA
    vmem = pl.BlockSpec(memory_space=pltpu.VMEM)
    smem = pl.BlockSpec(memory_space=pltpu.SMEM)
    held = [
        pltpu.with_memory_space_constraint(v, pltpu.HBM)
        for v in (tokens, teacher_protos, student_protos)
    ]
    hbm = pl.BlockSpec(memory_space=pltpu.HBM)
    out_base, proto_scale, token_scale, teacher_next = pl.pallas_call(
        functools.partial(sinkhorn_kernel, X, Y, Z),
        out_shape=(
            jax.ShapeDtypeStruct((Y, tdev, kb), F32),
            jax.ShapeDtypeStruct((Y, 1, kb), F32),
            jax.ShapeDtypeStruct((1, tdev), F32),
            jax.ShapeDtypeStruct(teacher_protos.shape, F32),
        ),
        in_specs=[smem, hbm, hbm, hbm],
        out_specs=(vmem, vmem, vmem, vmem),
        scratch_shapes=[
            pltpu.VMEM((tdev, width), BF16),
            pltpu.VMEM((1, kdev, width), F32),
            pltpu.VMEM((1, kdev, width), F32),
            pltpu.VMEM((Y, Z, 2, kdev, width), BF16),
            pltpu.VMEM((Z, 2, kdev, width), BF16),
            pltpu.VMEM((Y, tdev, width), BF16),
            pltpu.VMEM((tb, kb), BF16),
            pltpu.VMEM((ITERS, 2, 1, kb), F32),
            pltpu.VMEM((ITERS, 1, kb), F32),
            pltpu.VMEM((ITERS, Z - 1, 1, kb), F32),
            pltpu.VMEM((ITERS, 1, tb), F32),
            pltpu.VMEM((ITERS, X * Y - 1, 1, tb), F32),
            pltpu.VMEM((Y, 1, tdev), F32),
            dma((3,)), dma, dma, dma, dma, dma, dma,
            dma((ITERS,)), dma((ITERS,)), dma((ITERS,)), dma((ITERS,)), dma((ITERS,)), dma((ITERS,)),
            dma, dma,
            dma((n_ring,)), dma((n_ring,)), dma((n_ring,)), dma((n_ring,)),
        ],
        compiler_params=pltpu.CompilerParams(
            collective_id=0, has_side_effects=True, vmem_limit_bytes=32 * 2**20
        ),
        name="sinkhorn",
    )(momentum, *held)
    return pl.pallas_call(
        functools.partial(target_kernel, float(X * Y * kb)),
        grid=(Y,),
        out_shape=(
            jax.ShapeDtypeStruct(teacher_protos.shape, F32),
            jax.ShapeDtypeStruct((tdev, Y * kb), BF16),
        ),
        in_specs=[
            pl.BlockSpec((1, kdev, width), lambda i: (0, 0, 0)),
            pl.BlockSpec((1, tdev, kb), lambda i: (i, 0, 0)),
            pl.BlockSpec((1, 1, kb), lambda i: (i, 0, 0)),
            pl.BlockSpec((1, tdev), lambda i: (0, 0)),
        ],
        out_specs=(
            pl.BlockSpec((1, kdev, width), lambda i: (0, 0, 0)),
            pl.BlockSpec((tdev, kb), lambda i: (0, i)),
        ),
        scratch_shapes=[pltpu.VMEM((tdev, tdev), F32)],
        compiler_params=pltpu.CompilerParams(vmem_limit_bytes=32 * 2**20),
        name="targets",
    )(teacher_next, out_base, proto_scale, token_scale)


def build(mesh, X, Y, Z):
    return jax.shard_map(
        functools.partial(body, X, Y, Z),
        mesh=mesh,
        in_specs=(P("dp", None), P("proto", "dp", None), P("proto", "dp", None), P()),
        out_specs=(P("proto", "dp", None), P("dp", "proto")),
        check_vma=False,
    )


def solution(mesh):
    return build(mesh, mesh.shape["proto"], 8, mesh.shape["dp"] // 16)
```

```python
import functools

import jax
import jax.numpy as jnp
from jax import lax
from jax.experimental import pallas as pl
from jax.experimental.pallas import tpu as pltpu
from jax.sharding import PartitionSpec as P

ITERS = 3
TEACHER_TEMP = 0.07
MESH = pl.DeviceIdType.MESH
F32 = jnp.float32
BF16 = jnp.bfloat16


def unit_rows(m):
    return m / jnp.sqrt(jnp.sum(m * m, axis=-1, keepdims=True) + 1e-06)


def nt_dot(a, b):
    return lax.dot_general(a, b, (((1,), (1,)), ((), ())), preferred_element_type=F32)


def two_term_rows(v):
    n = v.shape[1]
    x = jnp.broadcast_to(v, (16, n))
    hi = x.astype(BF16).astype(F32)
    row = lax.broadcasted_iota(jnp.int32, (16, n), 0)
    return jnp.where(row == 0, hi, jnp.where(row == 1, x - hi, 0.0)).astype(BF16)


def packed(v, rows):
    n = v.shape[1] // 128
    parts = [v[:, i * 128 : (i + 1) * 128] for i in range(n)]
    if rows > n:
        parts.append(jnp.zeros((rows - n, 128), v.dtype))
    return jnp.concatenate(parts, axis=0)


def unpacked(v, n):
    return jnp.concatenate([v[i : i + 1] for i in range(n // 128)], axis=1)


def far_first(offsets, dist):
    return sorted(offsets, key=lambda o: (-dist(o), o))


def ring_dist(d, n):
    return min(d, n - d)


def sinkhorn_kernel(
    X, Y, Z,
    mom_ref, tok_hbm, tea_hbm, stu_hbm,
    out_base, ps_ref, ts_ref, next_ref,
    tok_ref, tea_ref, stu_ref, g_ref, pc, tc, base, csend, cpair, zsend, zbuf, rsend, xbuf, tbuf,
    in_sem, zg_send, zg_recv, tg_send, tg_recv, sf_send, sf_recv,
    c_send, c_recv, z_send, z_recv, r_send, r_recv, p_send, p_recv,
    ring_send, ring_recv, sib_send, sib_recv,
):
    x = lax.axis_index("proto")
    dp = lax.axis_index("dp")
    y, z, c = dp // (2 * Z), (dp // 2) % Z, dp % 2

    def at(xx, yy, zz, cc):
        return {"dp": (yy * Z + zz) * 2 + cc, "proto": xx}

    sibling = at(x, y, z, 1 - c)
    z_off = far_first(range(1, Z), lambda d: ring_dist(d, Z))
    y_off = far_first(range(1, Y), lambda d: ring_dist(d, Y))
    xy_off = far_first(
        [(dx, dy) for dx in range(X) for dy in range(Y) if (dx, dy) != (0, 0)],
        lambda o: ring_dist(o[0], X) + ring_dist(o[1], Y),
    )
    z_dev = [at(x, y, (z + d) % Z, c) for d in z_off]
    y_dev = [at(x, (y + d) % Y, z, c) for d in y_off]
    xy_dev = [at((x + dx) % X, (y + dy) % Y, z, c) for dx, dy in xy_off]

    loads = [
        pltpu.make_async_copy(src, dst, in_sem.at[i])
        for i, (src, dst) in enumerate([(tea_hbm, tea_ref), (stu_hbm, stu_ref), (tok_hbm, tok_ref)])
    ]
    for load in loads:
        load.start()

    barrier = pltpu.get_barrier_semaphore()
    far = lambda o: ring_dist(o[0], X) + ring_dist(o[1], Y) + ring_dist(o[2], Z)
    offsets = [(0, 0, d) for d in z_off] + [(dx, dy, 0) for dx, dy in xy_off]
    greeted = [
        at((x + dx) % X, (y + dy) % Y, (z + dz) % Z, c)
        for dx, dy, dz in sorted(offsets, key=lambda o: (-far(o), o))
    ] + [sibling]
    for d in greeted:
        pl.semaphore_signal(barrier, inc=1, device_id=d, device_id_type=MESH)

    keep = mom_ref[0]
    for load in loads:
        load.wait()
    teacher_next = keep * tea_ref[0] + (1.0 - keep) * stu_ref[0]
    next_ref[0] = teacher_next
    pc[z, c] = unit_rows(teacher_next).astype(BF16)
    tc[y] = unit_rows(tok_ref[...].astype(F32)).astype(BF16)
    pl.semaphore_wait(barrier, len(greeted))

    def send(src, dst, s, r, d):
        copy = pltpu.make_async_remote_copy(
            src_ref=src, dst_ref=dst, send_sem=s, recv_sem=r, device_id=d, device_id_type=MESH
        )
        copy.start()
        return copy

    def wait_bytes(ref, sem):
        pltpu.make_async_copy(ref, ref, sem).wait()

    for i in range(max(Z - 1, Y - 1)):
        if i < Z - 1:
            send(pc.at[z, c], pc.at[z, c], zg_send, zg_recv, z_dev[i])
        if i < Y - 1:
            send(tc.at[y], tc.at[y], tg_send, tg_recv, y_dev[i])
    wait_bytes(pc.at[0 : Z - 1, 0], zg_recv)
    swap = send(pc.at[:, c], pc.at[:, c], sf_send, sf_recv, sibling)

    up, down = at(x, (y + 1) % Y, z, c), at(x, (y + Y - 1) % Y, z, c)
    last, zh = Y // 2, Z // 2
    sends, sib = [], {}

    def ring_parts(s):
        if s < last:
            yield s - 1, up, (y - s + 1 + Y) % Y, (y - s + Y) % Y, slice(0, Z)
            yield last + s - 1, down, (y + s - 1) % Y, (y + s) % Y, slice(0, Z)
        elif s == last:
            yield s - 1, up, (y - s + 1 + Y) % Y, (y - s + Y) % Y, slice(0, zh)
            yield last + s - 1, down, (y + s - 1) % Y, (y + s) % Y, slice(zh, Z)

    def ring_step(s):
        for i, to, b, _, rows in ring_parts(s):
            src = pc.at[rows, c] if s == 1 else g_ref.at[b, rows, c]
            sends.append(send(src, g_ref.at[b, rows, c], ring_send.at[i], ring_recv.at[i], to))

    def ring_arrive(s):
        for i, _, _, b, rows in ring_parts(s):
            part = g_ref.at[b, rows, c]
            wait_bytes(part, ring_recv.at[i])
            sib[i] = send(part, part, sib_send.at[i], sib_recv.at[i], sibling)

    def ring_block(s):
        for i, _, _, b, _ in ring_parts(s):
            sib[i].wait_recv()
        for b in [(y - s + Y) % Y] * (s <= last) + [(y + s) % Y] * (s < last):
            block_base(b, g_ref[b])

    tdev = tc.shape[1]
    tb, kb = base.shape
    width = pc.shape[3]

    def block_base(b, block):
        scores = nt_dot(tc[y], block.reshape(kb, width))
        out_base[b] = jnp.exp(scores / TEACHER_TEMP)

    ring_step(1)
    wait_bytes(tc.at[0 : Y - 1], tg_recv)
    swap.wait_recv()
    protos = pc[...].reshape(kb, width)

    def score(i, acc):
        b = jnp.exp(nt_dot(tc[i], protos) / TEACHER_TEMP)
        base[pl.ds(pl.multiple_of(i * tdev, tdev), tdev), :] = b.astype(BF16)
        return acc + jnp.sum(b, axis=0, keepdims=True)

    cols = lax.fori_loop(0, Y, score, jnp.zeros((1, kb), F32))

    pairs = []
    for it in range(ITERS):
        csend[it] = packed(cols, csend.shape[1])
        pair = send(csend.at[it], cpair.at[it], c_send.at[it], c_recv.at[it], sibling)
        pair.wait_recv()
        zsend[it] = (csend[it] + cpair[it]).astype(BF16)
        for i, d in enumerate(z_dev):
            send(zsend.at[it], zbuf.at[it, i], z_send.at[it], z_recv.at[it], d)
        if it == 0:
            block_base(y, pc[...])
        if it == 1:
            ring_block(1)
        if it == 2:
            ring_arrive(3)
            ring_step(4)
            ring_block(2)
        wait_bytes(zbuf.at[it], z_recv.at[it])
        mass = zsend[it].astype(F32)
        for i in range(Z - 1):
            mass = mass + zbuf[it, i].astype(F32)
        protos_scale = unpacked(1.0 / mass, kb)
        rows = jnp.sum(nt_dot(two_term_rows(protos_scale), base[...]), axis=0, keepdims=True)
        rsend[it] = packed(rows, rsend.shape[1])
        for i, d in enumerate(xy_dev):
            send(rsend.at[it], xbuf.at[it, i], r_send.at[it], r_recv.at[it], d)
        if it == 1:
            ring_arrive(2)
            ring_step(3)
        if it == 2:
            ps_ref[y] = protos_scale
            for d in y_dev:
                send(ps_ref.at[y], ps_ref.at[y], p_send, p_recv, d)
            ring_arrive(4)
            ring_block(3)
            ring_block(4)
        wait_bytes(xbuf.at[it], r_recv.at[it])
        mass = rsend[it]
        for i in range(X * Y - 1):
            mass = mass + xbuf[it, i]
        token_scale = unpacked(1.0 / mass, tb)
        if it < ITERS - 1:
            cols = jnp.sum(
                jnp.dot(two_term_rows(token_scale), base[...], preferred_element_type=F32),
                axis=0,
                keepdims=True,
            )
            if it == 0:
                ring_arrive(1)
                ring_step(2)
        else:
            for i in range(Y):
                tbuf[i] = token_scale[:, i * tdev : (i + 1) * tdev]
            ts_ref[...] = tbuf[y]
        pairs.append(pair)

    wait_bytes(ps_ref.at[0 : Y - 1], p_recv)
    wait_bytes(ps_ref.at[0 : Y - 1], p_send)
    for it in range(ITERS):
        pairs[it].wait_send()
        wait_bytes(zbuf.at[it], z_send.at[it])
        wait_bytes(xbuf.at[it], r_send.at[it])
    wait_bytes(pc.at[0 : Z - 1, 0], zg_send)
    wait_bytes(tc.at[0 : Y - 1], tg_send)
    swap.wait_send()
    for copy in sends:
        copy.wait_send()
    for copy in sib.values():
        copy.wait_send()


def target_kernel(width, new_ref, base_ref, ps_ref, ts_ref, next_hbm, out_hbm, stage, sems):
    blocks, n, kb = base_ref.shape
    copies = [pltpu.make_async_copy(new_ref, next_hbm, sems.at[blocks])]
    copies[0].start()
    scale = jnp.transpose(jnp.broadcast_to(width * ts_ref[...], (n, n)))[:, 0:1]
    for b in range(blocks):
        stage[b] = (scale * base_ref[b] * ps_ref[b]).astype(BF16)
        copies.append(pltpu.make_async_copy(stage.at[b], out_hbm.at[:, b * kb : (b + 1) * kb], sems.at[b]))
        copies[-1].start()
    for copy in copies:
        copy.wait()


def body(X, Y, Z, tokens, teacher_protos, student_protos, momentum):
    tdev, width = tokens.shape
    kdev = teacher_protos.shape[1]
    kb, tb = 2 * Z * kdev, Y * tdev
    crows = -(-kb // 2048) * 16
    n_ring = 2 * (Y // 2)
    dma = pltpu.SemaphoreType.DMA
    vmem = pl.BlockSpec(memory_space=pltpu.VMEM)
    smem = pl.BlockSpec(memory_space=pltpu.SMEM)
    held = [
        pltpu.with_memory_space_constraint(v, pltpu.HBM)
        for v in (tokens, teacher_protos, student_protos)
    ]
    hbm = pl.BlockSpec(memory_space=pltpu.HBM)
    out_base, proto_scale, token_scale, teacher_next = pl.pallas_call(
        functools.partial(sinkhorn_kernel, X, Y, Z),
        out_shape=(
            jax.ShapeDtypeStruct((Y, tdev, kb), F32),
            jax.ShapeDtypeStruct((Y, 1, kb), F32),
            jax.ShapeDtypeStruct((1, tdev), F32),
            jax.ShapeDtypeStruct(teacher_protos.shape, F32),
        ),
        in_specs=[smem, hbm, hbm, hbm],
        out_specs=(vmem, vmem, vmem, vmem),
        scratch_shapes=[
            pltpu.VMEM((tdev, width), BF16),
            pltpu.VMEM((1, kdev, width), F32),
            pltpu.VMEM((1, kdev, width), F32),
            pltpu.VMEM((Y, Z, 2, kdev, width), BF16),
            pltpu.VMEM((Z, 2, kdev, width), BF16),
            pltpu.VMEM((Y, tdev, width), BF16),
            pltpu.VMEM((tb, kb), BF16),
            pltpu.VMEM((ITERS, crows, 128), F32),
            pltpu.VMEM((ITERS, crows, 128), F32),
            pltpu.VMEM((ITERS, crows, 128), BF16),
            pltpu.VMEM((ITERS, Z - 1, crows, 128), BF16),
            pltpu.VMEM((ITERS, tb // 128, 128), F32),
            pltpu.VMEM((ITERS, X * Y - 1, tb // 128, 128), F32),
            pltpu.VMEM((Y, 1, tdev), F32),
            dma((3,)), dma, dma, dma, dma, dma, dma,
            dma((ITERS,)), dma((ITERS,)), dma((ITERS,)), dma((ITERS,)), dma((ITERS,)), dma((ITERS,)),
            dma, dma,
            dma((n_ring,)), dma((n_ring,)), dma((n_ring,)), dma((n_ring,)),
        ],
        compiler_params=pltpu.CompilerParams(
            collective_id=0, has_side_effects=True, vmem_limit_bytes=32 * 2**20
        ),
        name="sinkhorn",
    )(momentum, *held)
    return pl.pallas_call(
        functools.partial(target_kernel, float(X * Y * kb)),
        out_shape=(
            jax.ShapeDtypeStruct(teacher_protos.shape, F32),
            jax.ShapeDtypeStruct((tdev, Y * kb), BF16),
        ),
        in_specs=[vmem, vmem, vmem, vmem],
        out_specs=(hbm, hbm),
        scratch_shapes=[pltpu.VMEM((Y, tdev, kb), BF16), dma((Y + 1,))],
        compiler_params=pltpu.CompilerParams(vmem_limit_bytes=32 * 2**20),
        name="targets",
    )(teacher_next, out_base, proto_scale, token_scale)


def build(mesh, X, Y, Z):
    return jax.shard_map(
        functools.partial(body, X, Y, Z),
        mesh=mesh,
        in_specs=(P("dp", None), P("proto", "dp", None), P("proto", "dp", None), P()),
        out_specs=(P("proto", "dp", None), P("dp", "proto")),
        check_vma=False,
    )


def solution(mesh):
    return build(mesh, mesh.shape["proto"], 8, mesh.shape["dp"] // 16)
```

```python
import functools

import jax
import jax.numpy as jnp
from jax import lax
from jax.experimental import pallas as pl
from jax.experimental.pallas import tpu as pltpu
from jax.sharding import PartitionSpec as P

ITERS = 3
TEACHER_TEMP = 0.07
MESH = pl.DeviceIdType.MESH
F32 = jnp.float32
BF16 = jnp.bfloat16


def unit_rows(m):
    return m / jnp.sqrt(jnp.sum(m * m, axis=-1, keepdims=True) + 1e-06)


def nt_dot(a, b):
    return lax.dot_general(a, b, (((1,), (1,)), ((), ())), preferred_element_type=F32)


def two_term_rows(v):
    n = v.shape[1]
    x = jnp.broadcast_to(v, (16, n))
    hi = x.astype(BF16).astype(F32)
    row = lax.broadcasted_iota(jnp.int32, (16, n), 0)
    return jnp.where(row == 0, hi, jnp.where(row == 1, x - hi, 0.0)).astype(BF16)


def packed(v, rows):
    n = v.shape[1] // 128
    parts = [v[:, i * 128 : (i + 1) * 128] for i in range(n)]
    if rows > n:
        parts.append(jnp.zeros((rows - n, 128), v.dtype))
    return jnp.concatenate(parts, axis=0)


def unpacked(v, n):
    return jnp.concatenate([v[i : i + 1] for i in range(n // 128)], axis=1)


def far_first(offsets, dist):
    return sorted(offsets, key=lambda o: (-dist(o), o))


def ring_dist(d, n):
    return min(d, n - d)


def sinkhorn_kernel(
    X, Y, Z,
    mom_ref, tok_hbm, tea_hbm, stu_hbm,
    out_base, ps_ref, ts_ref, next_ref,
    tok_ref, tea_ref, stu_ref, g_ref, pc, tc, base, csend, cpair, zsend, zbuf, rsend, xbuf, tbuf,
    in_sem, zg_send, zg_recv, tg_send, tg_recv, sf_send, sf_recv,
    c_send, c_recv, z_send, z_recv, r_send, r_recv, p_send, p_recv,
    ring_send, ring_recv, sib_send, sib_recv,
):
    x = lax.axis_index("proto")
    dp = lax.axis_index("dp")
    y, z, c = dp // (2 * Z), (dp // 2) % Z, dp % 2

    def at(xx, yy, zz, cc):
        return {"dp": (yy * Z + zz) * 2 + cc, "proto": xx}

    sibling = at(x, y, z, 1 - c)
    z_off = far_first(range(1, Z), lambda d: ring_dist(d, Z))
    y_off = far_first(range(1, Y), lambda d: ring_dist(d, Y))
    xy_off = far_first(
        [(dx, dy) for dx in range(X) for dy in range(Y) if (dx, dy) != (0, 0)],
        lambda o: ring_dist(o[0], X) + ring_dist(o[1], Y),
    )
    z_dev = [at(x, y, (z + d) % Z, c) for d in z_off]
    y_dev = [at(x, (y + d) % Y, z, c) for d in y_off]
    xy_dev = [at((x + dx) % X, (y + dy) % Y, z, c) for dx, dy in xy_off]

    loads = [
        pltpu.make_async_copy(src, dst, in_sem.at[i])
        for i, (src, dst) in enumerate([(tea_hbm, tea_ref), (stu_hbm, stu_ref), (tok_hbm, tok_ref)])
    ]
    for load in loads:
        load.start()

    barrier = pltpu.get_barrier_semaphore()
    far = lambda o: ring_dist(o[0], X) + ring_dist(o[1], Y) + ring_dist(o[2], Z)
    offsets = [(0, 0, d) for d in z_off] + [(dx, dy, 0) for dx, dy in xy_off]
    greeted = [
        at((x + dx) % X, (y + dy) % Y, (z + dz) % Z, c)
        for dx, dy, dz in sorted(offsets, key=lambda o: (-far(o), o))
    ] + [sibling]
    for d in greeted:
        pl.semaphore_signal(barrier, inc=1, device_id=d, device_id_type=MESH)

    keep = mom_ref[0]
    for load in loads:
        load.wait()
    teacher_next = keep * tea_ref[0] + (1.0 - keep) * stu_ref[0]
    next_ref[0] = teacher_next
    pc[z, c] = unit_rows(teacher_next).astype(BF16)
    tc[y] = unit_rows(tok_ref[...].astype(F32)).astype(BF16)
    pl.semaphore_wait(barrier, len(greeted))

    def send(src, dst, s, r, d):
        copy = pltpu.make_async_remote_copy(
            src_ref=src, dst_ref=dst, send_sem=s, recv_sem=r, device_id=d, device_id_type=MESH
        )
        copy.start()
        return copy

    def wait_bytes(ref, sem):
        pltpu.make_async_copy(ref, ref, sem).wait()

    for i in range(max(Z - 1, Y - 1)):
        if i < Z - 1:
            send(pc.at[z, c], pc.at[z, c], zg_send, zg_recv, z_dev[i])
        if i < Y - 1:
            send(tc.at[y], tc.at[y], tg_send, tg_recv, y_dev[i])
    wait_bytes(pc.at[0 : Z - 1, 0], zg_recv)
    swap = send(pc.at[:, c], pc.at[:, c], sf_send, sf_recv, sibling)

    up, down = at(x, (y + 1) % Y, z, c), at(x, (y + Y - 1) % Y, z, c)
    last, zh = Y // 2, Z // 2
    sends, sib = [], {}

    def ring_parts(s):
        if s < last:
            yield s - 1, up, (y - s + 1 + Y) % Y, (y - s + Y) % Y, slice(0, Z)
            yield last + s - 1, down, (y + s - 1) % Y, (y + s) % Y, slice(0, Z)
        elif s == last:
            yield s - 1, up, (y - s + 1 + Y) % Y, (y - s + Y) % Y, slice(0, zh)
            yield last + s - 1, down, (y + s - 1) % Y, (y + s) % Y, slice(zh, Z)

    def ring_step(s):
        for i, to, b, _, rows in ring_parts(s):
            src = pc.at[rows, c] if s == 1 else g_ref.at[b, rows, c]
            sends.append(send(src, g_ref.at[b, rows, c], ring_send.at[i], ring_recv.at[i], to))

    def ring_arrive(s):
        for i, _, _, b, rows in ring_parts(s):
            part = g_ref.at[b, rows, c]
            wait_bytes(part, ring_recv.at[i])
            sib[i] = send(part, part, sib_send.at[i], sib_recv.at[i], sibling)

    def ring_block(s):
        for i, _, _, b, _ in ring_parts(s):
            sib[i].wait_recv()
        for b in [(y - s + Y) % Y] * (s <= last) + [(y + s) % Y] * (s < last):
            block_base(b, g_ref[b])

    tdev = tc.shape[1]
    tb, kb = base.shape
    width = pc.shape[3]

    def block_base(b, block):
        scores = nt_dot(tc[y], block.reshape(kb, width))
        out_base[b] = jnp.exp(scores / TEACHER_TEMP)

    ring_step(1)
    wait_bytes(tc.at[0 : Y - 1], tg_recv)
    swap.wait_recv()
    protos = pc[...].reshape(kb, width)

    b = jnp.exp(nt_dot(tc[...].reshape(tb, width), protos) / TEACHER_TEMP)
    base[...] = b.astype(BF16)
    cols = jnp.sum(b, axis=0, keepdims=True)

    pairs = []
    for it in range(ITERS):
        csend[it] = packed(cols, csend.shape[1])
        pair = send(csend.at[it], cpair.at[it], c_send.at[it], c_recv.at[it], sibling)
        pair.wait_recv()
        zsend[it] = (csend[it] + cpair[it]).astype(BF16)
        for i, d in enumerate(z_dev):
            send(zsend.at[it], zbuf.at[it, i], z_send.at[it], z_recv.at[it], d)
        if it == 0:
            block_base(y, pc[...])
        if it == 1:
            ring_block(1)
        if it == 2:
            ring_block(2)
            ring_arrive(3)
            ring_step(4)
        wait_bytes(zbuf.at[it], z_recv.at[it])
        mass = zsend[it].astype(F32)
        for i in range(Z - 1):
            mass = mass + zbuf[it, i].astype(F32)
        protos_scale = unpacked(1.0 / mass, kb)
        rows = jnp.sum(nt_dot(two_term_rows(protos_scale), base[...]), axis=0, keepdims=True)
        rsend[it] = packed(rows, rsend.shape[1])
        for i, d in enumerate(xy_dev):
            send(rsend.at[it], xbuf.at[it, i], r_send.at[it], r_recv.at[it], d)
        if it == 1:
            ring_arrive(2)
            ring_step(3)
        if it == 2:
            ps_ref[y] = protos_scale
            for d in y_dev:
                send(ps_ref.at[y], ps_ref.at[y], p_send, p_recv, d)
            ring_block(3)
            ring_arrive(4)
            ring_block(4)
        wait_bytes(xbuf.at[it], r_recv.at[it])
        mass = rsend[it]
        for i in range(X * Y - 1):
            mass = mass + xbuf[it, i]
        token_scale = unpacked(1.0 / mass, tb)
        if it < ITERS - 1:
            cols = jnp.sum(
                jnp.dot(two_term_rows(token_scale), base[...], preferred_element_type=F32),
                axis=0,
                keepdims=True,
            )
            if it == 0:
                ring_arrive(1)
                ring_step(2)
        else:
            for i in range(Y):
                tbuf[i] = token_scale[:, i * tdev : (i + 1) * tdev]
            ts_ref[...] = tbuf[y]
        pairs.append(pair)

    wait_bytes(ps_ref.at[0 : Y - 1], p_recv)
    wait_bytes(ps_ref.at[0 : Y - 1], p_send)
    for it in range(ITERS):
        pairs[it].wait_send()
        wait_bytes(zbuf.at[it], z_send.at[it])
        wait_bytes(xbuf.at[it], r_send.at[it])
    wait_bytes(pc.at[0 : Z - 1, 0], zg_send)
    wait_bytes(tc.at[0 : Y - 1], tg_send)
    swap.wait_send()
    for copy in sends:
        copy.wait_send()
    for copy in sib.values():
        copy.wait_send()


def target_kernel(width, new_ref, base_ref, ps_ref, ts_ref, next_hbm, out_hbm, stage, sems):
    blocks, n, kb = base_ref.shape
    copies = [pltpu.make_async_copy(new_ref, next_hbm, sems.at[blocks])]
    copies[0].start()
    scale = jnp.transpose(jnp.broadcast_to(width * ts_ref[...], (n, n)))[:, 0:1]
    for b in range(blocks):
        stage[b] = (scale * base_ref[b] * ps_ref[b]).astype(BF16)
        copies.append(pltpu.make_async_copy(stage.at[b], out_hbm.at[:, b * kb : (b + 1) * kb], sems.at[b]))
        copies[-1].start()
    for copy in copies:
        copy.wait()


def body(X, Y, Z, tokens, teacher_protos, student_protos, momentum):
    tdev, width = tokens.shape
    kdev = teacher_protos.shape[1]
    kb, tb = 2 * Z * kdev, Y * tdev
    crows = -(-kb // 2048) * 16
    n_ring = 2 * (Y // 2)
    dma = pltpu.SemaphoreType.DMA
    vmem = pl.BlockSpec(memory_space=pltpu.VMEM)
    smem = pl.BlockSpec(memory_space=pltpu.SMEM)
    held = [
        pltpu.with_memory_space_constraint(v, pltpu.HBM)
        for v in (tokens, teacher_protos, student_protos)
    ]
    hbm = pl.BlockSpec(memory_space=pltpu.HBM)
    out_base, proto_scale, token_scale, teacher_next = pl.pallas_call(
        functools.partial(sinkhorn_kernel, X, Y, Z),
        out_shape=(
            jax.ShapeDtypeStruct((Y, tdev, kb), F32),
            jax.ShapeDtypeStruct((Y, 1, kb), F32),
            jax.ShapeDtypeStruct((1, tdev), F32),
            jax.ShapeDtypeStruct(teacher_protos.shape, F32),
        ),
        in_specs=[smem, hbm, hbm, hbm],
        out_specs=(vmem, vmem, vmem, vmem),
        scratch_shapes=[
            pltpu.VMEM((tdev, width), BF16),
            pltpu.VMEM((1, kdev, width), F32),
            pltpu.VMEM((1, kdev, width), F32),
            pltpu.VMEM((Y, Z, 2, kdev, width), BF16),
            pltpu.VMEM((Z, 2, kdev, width), BF16),
            pltpu.VMEM((Y, tdev, width), BF16),
            pltpu.VMEM((tb, kb), BF16),
            pltpu.VMEM((ITERS, crows, 128), F32),
            pltpu.VMEM((ITERS, crows, 128), F32),
            pltpu.VMEM((ITERS, crows, 128), BF16),
            pltpu.VMEM((ITERS, Z - 1, crows, 128), BF16),
            pltpu.VMEM((ITERS, tb // 128, 128), F32),
            pltpu.VMEM((ITERS, X * Y - 1, tb // 128, 128), F32),
            pltpu.VMEM((Y, 1, tdev), F32),
            dma((3,)), dma, dma, dma, dma, dma, dma,
            dma((ITERS,)), dma((ITERS,)), dma((ITERS,)), dma((ITERS,)), dma((ITERS,)), dma((ITERS,)),
            dma, dma,
            dma((n_ring,)), dma((n_ring,)), dma((n_ring,)), dma((n_ring,)),
        ],
        compiler_params=pltpu.CompilerParams(
            collective_id=0, has_side_effects=True, vmem_limit_bytes=32 * 2**20
        ),
        name="sinkhorn",
    )(momentum, *held)
    return pl.pallas_call(
        functools.partial(target_kernel, float(X * Y * kb)),
        out_shape=(
            jax.ShapeDtypeStruct(teacher_protos.shape, F32),
            jax.ShapeDtypeStruct((tdev, Y * kb), BF16),
        ),
        in_specs=[vmem, vmem, vmem, vmem],
        out_specs=(hbm, hbm),
        scratch_shapes=[pltpu.VMEM((Y, tdev, kb), BF16), dma((Y + 1,))],
        compiler_params=pltpu.CompilerParams(vmem_limit_bytes=32 * 2**20),
        name="targets",
    )(teacher_next, out_base, proto_scale, token_scale)


def build(mesh, X, Y, Z):
    return jax.shard_map(
        functools.partial(body, X, Y, Z),
        mesh=mesh,
        in_specs=(P("dp", None), P("proto", "dp", None), P("proto", "dp", None), P()),
        out_specs=(P("proto", "dp", None), P("dp", "proto")),
        check_vma=False,
    )


def solution(mesh):
    return build(mesh, mesh.shape["proto"], 8, mesh.shape["dp"] // 16)
```

```python
import functools
import math

import jax
import jax.numpy as jnp
from jax import lax
from jax.experimental import pallas as pl
from jax.experimental.pallas import tpu as pltpu
from jax.sharding import PartitionSpec as P

ITERS = 3
TEACHER_TEMP = 0.07
EXP2_RATE = math.log2(math.e) / TEACHER_TEMP
MESH = pl.DeviceIdType.MESH
F32 = jnp.float32
BF16 = jnp.bfloat16


def unit_rows(m):
    return m / jnp.sqrt(jnp.sum(m * m, axis=-1, keepdims=True) + 1e-06)


def nt_dot(a, b):
    return lax.dot_general(a, b, (((1,), (1,)), ((), ())), preferred_element_type=F32)


def two_term_rows(v):
    n = v.shape[1]
    x = jnp.broadcast_to(v, (16, n))
    hi = x.astype(BF16).astype(F32)
    row = lax.broadcasted_iota(jnp.int32, (16, n), 0)
    return jnp.where(row == 0, hi, jnp.where(row == 1, x - hi, 0.0)).astype(BF16)


def packed(v, rows):
    n = v.shape[1] // 128
    parts = [v[:, i * 128 : (i + 1) * 128] for i in range(n)]
    if rows > n:
        parts.append(jnp.zeros((rows - n, 128), v.dtype))
    return jnp.concatenate(parts, axis=0)


def unpacked(v, n):
    return jnp.concatenate([v[i : i + 1] for i in range(n // 128)], axis=1)


def far_first(offsets, dist):
    return sorted(offsets, key=lambda o: (-dist(o), o))


def ring_dist(d, n):
    return min(d, n - d)


def sinkhorn_kernel(
    X, Y, Z,
    mom_ref, tok_hbm, tea_hbm, stu_hbm,
    out_base, ps_ref, ts_ref, next_ref,
    tok_ref, tea_ref, stu_ref, g_ref, pc, tc, base, csend, cpair, zsend, zbuf, rsend, xbuf, tbuf,
    in_sem, zg_send, zg_recv, tg_send, tg_recv, sf_send, sf_recv,
    c_send, c_recv, z_send, z_recv, r_send, r_recv, p_send, p_recv,
    ring_send, ring_recv, sib_send, sib_recv,
):
    x = lax.axis_index("proto")
    dp = lax.axis_index("dp")
    y, z, c = dp // (2 * Z), (dp // 2) % Z, dp % 2

    def at(xx, yy, zz, cc):
        return {"dp": (yy * Z + zz) * 2 + cc, "proto": xx}

    sibling = at(x, y, z, 1 - c)
    z_off = far_first(range(1, Z), lambda d: ring_dist(d, Z))
    y_off = far_first(range(1, Y), lambda d: ring_dist(d, Y))
    xy_off = far_first(
        [(dx, dy) for dx in range(X) for dy in range(Y) if (dx, dy) != (0, 0)],
        lambda o: ring_dist(o[0], X) + ring_dist(o[1], Y),
    )
    z_dev = [at(x, y, (z + d) % Z, c) for d in z_off]
    y_dev = [at(x, (y + d) % Y, z, c) for d in y_off]
    xy_dev = [at((x + dx) % X, (y + dy) % Y, z, c) for dx, dy in xy_off]

    loads = [
        pltpu.make_async_copy(src, dst, in_sem.at[i])
        for i, (src, dst) in enumerate([(tea_hbm, tea_ref), (stu_hbm, stu_ref), (tok_hbm, tok_ref)])
    ]
    for load in loads:
        load.start()

    barrier = pltpu.get_barrier_semaphore()
    far = lambda o: ring_dist(o[0], X) + ring_dist(o[1], Y) + ring_dist(o[2], Z)
    offsets = [(0, 0, d) for d in z_off] + [(dx, dy, 0) for dx, dy in xy_off]
    greeted = [
        at((x + dx) % X, (y + dy) % Y, (z + dz) % Z, c)
        for dx, dy, dz in sorted(offsets, key=lambda o: (-far(o), o))
    ] + [sibling]
    for d in greeted:
        pl.semaphore_signal(barrier, inc=1, device_id=d, device_id_type=MESH)

    keep = mom_ref[0]
    for load in loads:
        load.wait()
    teacher_next = keep * tea_ref[0] + (1.0 - keep) * stu_ref[0]
    next_ref[0] = teacher_next
    pc[z, c] = unit_rows(teacher_next).astype(BF16)
    tc[y] = unit_rows(tok_ref[...].astype(F32)).astype(BF16)
    pl.semaphore_wait(barrier, len(greeted))

    def send(src, dst, s, r, d):
        copy = pltpu.make_async_remote_copy(
            src_ref=src, dst_ref=dst, send_sem=s, recv_sem=r, device_id=d, device_id_type=MESH
        )
        copy.start()
        return copy

    def wait_bytes(ref, sem):
        pltpu.make_async_copy(ref, ref, sem).wait()

    for i in range(max(Z - 1, Y - 1)):
        if i < Z - 1:
            send(pc.at[z, c], pc.at[z, c], zg_send, zg_recv, z_dev[i])
        if i < Y - 1:
            send(tc.at[y], tc.at[y], tg_send, tg_recv, y_dev[i])
    wait_bytes(pc.at[0 : Z - 1, 0], zg_recv)
    swap = send(pc.at[:, c], pc.at[:, c], sf_send, sf_recv, sibling)

    up, down = at(x, (y + 1) % Y, z, c), at(x, (y + Y - 1) % Y, z, c)
    last, zh = Y // 2, Z // 2
    sends, sib = [], {}

    def ring_parts(s):
        if s < last:
            yield s - 1, up, (y - s + 1 + Y) % Y, (y - s + Y) % Y, slice(0, Z)
            yield last + s - 1, down, (y + s - 1) % Y, (y + s) % Y, slice(0, Z)
        elif s == last:
            yield s - 1, up, (y - s + 1 + Y) % Y, (y - s + Y) % Y, slice(0, zh)
            yield last + s - 1, down, (y + s - 1) % Y, (y + s) % Y, slice(zh, Z)

    def ring_step(s):
        for i, to, b, _, rows in ring_parts(s):
            src = pc.at[rows, c] if s == 1 else g_ref.at[b, rows, c]
            sends.append(send(src, g_ref.at[b, rows, c], ring_send.at[i], ring_recv.at[i], to))

    def ring_arrive(s):
        for i, _, _, b, rows in ring_parts(s):
            part = g_ref.at[b, rows, c]
            wait_bytes(part, ring_recv.at[i])
            sib[i] = send(part, part, sib_send.at[i], sib_recv.at[i], sibling)

    def ring_block(s):
        for i, _, _, b, _ in ring_parts(s):
            sib[i].wait_recv()
        for b in [(y - s + Y) % Y] * (s <= last) + [(y + s) % Y] * (s < last):
            block_base(b, g_ref[b])

    tdev = tc.shape[1]
    tb, kb = base.shape
    width = pc.shape[3]

    def block_base(b, block):
        scores = nt_dot(tc[y], block.reshape(kb, width))
        out_base[b] = jnp.exp2(scores * EXP2_RATE)

    ring_step(1)
    wait_bytes(tc.at[0 : Y - 1], tg_recv)
    swap.wait_recv()
    protos = pc[...].reshape(kb, width)

    b = jnp.exp2(nt_dot(tc[...].reshape(tb, width), protos) * EXP2_RATE)
    base[...] = b.astype(BF16)
    cols = jnp.sum(b, axis=0, keepdims=True)

    pairs = []
    for it in range(ITERS):
        csend[it] = packed(cols, csend.shape[1])
        pair = send(csend.at[it], cpair.at[it], c_send.at[it], c_recv.at[it], sibling)
        pair.wait_recv()
        zsend[it] = (csend[it] + cpair[it]).astype(BF16)
        for i, d in enumerate(z_dev):
            send(zsend.at[it], zbuf.at[it, i], z_send.at[it], z_recv.at[it], d)
        if it == 0:
            block_base(y, pc[...])
        if it == 1:
            ring_block(1)
        if it == 2:
            ring_block(2)
            ring_arrive(3)
            ring_step(4)
        wait_bytes(zbuf.at[it], z_recv.at[it])
        mass = zsend[it].astype(F32)
        for i in range(Z - 1):
            mass = mass + zbuf[it, i].astype(F32)
        protos_scale = unpacked(1.0 / mass, kb)
        rows = jnp.sum(nt_dot(two_term_rows(protos_scale), base[...]), axis=0, keepdims=True)
        rsend[it] = packed(rows, rsend.shape[1])
        for i, d in enumerate(xy_dev):
            send(rsend.at[it], xbuf.at[it, i], r_send.at[it], r_recv.at[it], d)
        if it == 1:
            ring_arrive(2)
            ring_step(3)
        if it == 2:
            ps_ref[y] = protos_scale
            for d in y_dev:
                send(ps_ref.at[y], ps_ref.at[y], p_send, p_recv, d)
            ring_block(3)
            ring_arrive(4)
            ring_block(4)
        wait_bytes(xbuf.at[it], r_recv.at[it])
        mass = rsend[it]
        for i in range(X * Y - 1):
            mass = mass + xbuf[it, i]
        token_scale = unpacked(1.0 / mass, tb)
        if it < ITERS - 1:
            cols = jnp.sum(
                jnp.dot(two_term_rows(token_scale), base[...], preferred_element_type=F32),
                axis=0,
                keepdims=True,
            )
            if it == 0:
                ring_arrive(1)
                ring_step(2)
        else:
            for i in range(Y):
                tbuf[i] = token_scale[:, i * tdev : (i + 1) * tdev]
            ts_ref[...] = tbuf[y]
        pairs.append(pair)

    wait_bytes(ps_ref.at[0 : Y - 1], p_recv)
    wait_bytes(ps_ref.at[0 : Y - 1], p_send)
    for it in range(ITERS):
        pairs[it].wait_send()
        wait_bytes(zbuf.at[it], z_send.at[it])
        wait_bytes(xbuf.at[it], r_send.at[it])
    wait_bytes(pc.at[0 : Z - 1, 0], zg_send)
    wait_bytes(tc.at[0 : Y - 1], tg_send)
    swap.wait_send()
    for copy in sends:
        copy.wait_send()
    for copy in sib.values():
        copy.wait_send()


def target_kernel(width, new_ref, base_ref, ps_ref, ts_ref, next_hbm, out_hbm, stage, sems):
    blocks, n, kb = base_ref.shape
    copies = [pltpu.make_async_copy(new_ref, next_hbm, sems.at[blocks])]
    copies[0].start()
    scale = jnp.transpose(jnp.broadcast_to(width * ts_ref[...], (n, n)))[:, 0:1]
    for b in range(blocks):
        stage[b] = (scale * base_ref[b] * ps_ref[b]).astype(BF16)
        copies.append(pltpu.make_async_copy(stage.at[b], out_hbm.at[:, b * kb : (b + 1) * kb], sems.at[b]))
        copies[-1].start()
    for copy in copies:
        copy.wait()


def body(X, Y, Z, tokens, teacher_protos, student_protos, momentum):
    tdev, width = tokens.shape
    kdev = teacher_protos.shape[1]
    kb, tb = 2 * Z * kdev, Y * tdev
    crows = -(-kb // 2048) * 16
    n_ring = 2 * (Y // 2)
    dma = pltpu.SemaphoreType.DMA
    vmem = pl.BlockSpec(memory_space=pltpu.VMEM)
    smem = pl.BlockSpec(memory_space=pltpu.SMEM)
    held = [
        pltpu.with_memory_space_constraint(v, pltpu.HBM)
        for v in (tokens, teacher_protos, student_protos)
    ]
    hbm = pl.BlockSpec(memory_space=pltpu.HBM)
    out_base, proto_scale, token_scale, teacher_next = pl.pallas_call(
        functools.partial(sinkhorn_kernel, X, Y, Z),
        out_shape=(
            jax.ShapeDtypeStruct((Y, tdev, kb), F32),
            jax.ShapeDtypeStruct((Y, 1, kb), F32),
            jax.ShapeDtypeStruct((1, tdev), F32),
            jax.ShapeDtypeStruct(teacher_protos.shape, F32),
        ),
        in_specs=[smem, hbm, hbm, hbm],
        out_specs=(vmem, vmem, vmem, vmem),
        scratch_shapes=[
            pltpu.VMEM((tdev, width), BF16),
            pltpu.VMEM((1, kdev, width), F32),
            pltpu.VMEM((1, kdev, width), F32),
            pltpu.VMEM((Y, Z, 2, kdev, width), BF16),
            pltpu.VMEM((Z, 2, kdev, width), BF16),
            pltpu.VMEM((Y, tdev, width), BF16),
            pltpu.VMEM((tb, kb), BF16),
            pltpu.VMEM((ITERS, crows, 128), F32),
            pltpu.VMEM((ITERS, crows, 128), F32),
            pltpu.VMEM((ITERS, crows, 128), BF16),
            pltpu.VMEM((ITERS, Z - 1, crows, 128), BF16),
            pltpu.VMEM((ITERS, tb // 128, 128), F32),
            pltpu.VMEM((ITERS, X * Y - 1, tb // 128, 128), F32),
            pltpu.VMEM((Y, 1, tdev), F32),
            dma((3,)), dma, dma, dma, dma, dma, dma,
            dma((ITERS,)), dma((ITERS,)), dma((ITERS,)), dma((ITERS,)), dma((ITERS,)), dma((ITERS,)),
            dma, dma,
            dma((n_ring,)), dma((n_ring,)), dma((n_ring,)), dma((n_ring,)),
        ],
        compiler_params=pltpu.CompilerParams(
            collective_id=0, has_side_effects=True, vmem_limit_bytes=32 * 2**20
        ),
        name="sinkhorn",
    )(momentum, *held)
    return pl.pallas_call(
        functools.partial(target_kernel, float(X * Y * kb)),
        out_shape=(
            jax.ShapeDtypeStruct(teacher_protos.shape, F32),
            jax.ShapeDtypeStruct((tdev, Y * kb), BF16),
        ),
        in_specs=[vmem, vmem, vmem, vmem],
        out_specs=(hbm, hbm),
        scratch_shapes=[pltpu.VMEM((Y, tdev, kb), BF16), dma((Y + 1,))],
        compiler_params=pltpu.CompilerParams(vmem_limit_bytes=32 * 2**20),
        name="targets",
    )(teacher_next, out_base, proto_scale, token_scale)


def build(mesh, X, Y, Z):
    return jax.shard_map(
        functools.partial(body, X, Y, Z),
        mesh=mesh,
        in_specs=(P("dp", None), P("proto", "dp", None), P("proto", "dp", None), P()),
        out_specs=(P("proto", "dp", None), P("dp", "proto")),
        check_vma=False,
    )


def solution(mesh):
    return build(mesh, mesh.shape["proto"], 8, mesh.shape["dp"] // 16)
```
